32 devices in a mesh: tmpl: 8 (over y, x, core), sta: 4 (over z).
Axes of the slice: x: 2, y: 2, z: 4, core: 2. Of those that a mesh axis runs over, the one named last changes fastest.
Arguments:
- window: bfloat16 [300, 1024], P('sta', 'tmpl'), may hold values from -6 to 6
- library: bfloat16 [64, 300, 300], P(None, 'sta'), may hold values from -6 to 6
- library_index: int32 [8], P('tmpl'), may hold values from 0 to 63
- moveout: int32 [8, 300], P('tmpl', 'sta'), may hold values from 0 to 212, as said below
- group_of: int32 [300], P('sta'), may hold values from 0 to 15, never falling along the last dimension, each value on 1 to 32 neighbouring positions
Outputs:
- stacks: bfloat16 [8, 16, 512], P('tmpl', None, 'sta')
The draws below stay inside these ranges and needn't reach their ends.
Inputs may be any that keep to these rules, and one draw needn't show every extreme that they name: Every row of moveout has some channel at 0 and some channel at 212.
All inputs are finite; a program needn't handle non-finite values.
Results may differ from the reference program's by a relative error of at most 0.01.
Values may be sent and summed in bfloat16 or wider, within the bound.
A program may use at most 128 MiB of HBM per device.

```python
import math
import jax
import jax.numpy as jnp
import numpy as np
from jax import lax

CHANNELS = 300
TMPL_LEN = 300
MAX_SHIFT = 212
LIBRARY = 64
GROUPS = 16
GROUP_MOST = 32
TEMPLATES = 8
WINDOW = 1024
LAG_COUNT = 512
N_STA = 4


def draw_moveout(key, part):
    raw = jax.random.randint(key, (TEMPLATES, CHANNELS), 0, MAX_SHIFT + 1)
    rows = jnp.arange(TEMPLATES, dtype=jnp.int32)[:, None]
    columns = jnp.arange(CHANNELS, dtype=jnp.int32)[None, :]
    lowest = columns == rows % CHANNELS
    highest = columns == (rows + 1) % CHANNELS
    shifted = jnp.where(highest, MAX_SHIFT, raw)
    return jnp.where(lowest, 0, shifted).astype(jnp.int32)


def set_ends(array, key, low, top_value):
    longest = array.shape.index(max(array.shape))
    spots = []
    for shift in (0, 1):
        where = [jax.random.randint(jax.random.fold_in(key, axis), (), 0, length) for axis, length in enumerate(array.shape)]
        where[longest] = (where[longest] + shift) % array.shape[longest]
        spots.append(tuple(where))
    return array.at[spots[0]].set(low).at[spots[1]].set(top_value)


def levels(rng, dims, cuts, smallest, top_value):
    gain = 1.0
    for dim, shards_of in cuts:
        heights = jax.random.uniform(jax.random.fold_in(jax.random.fold_in(rng, 6), dim), (shards_of,), jnp.float32, smallest / len(cuts), top_value / len(cuts))
        gain = gain * jnp.repeat(jnp.exp(heights), dims[dim] // shards_of).reshape((-1,) + (1,) * (len(dims) - 1 - dim))
    return gain


def profile(count, total, most, skew):
    portions = [(1 << 20) // math.isqrt(rank ** skew) + 1 for rank in range(2, count + 1)]
    spare, holding = total - most - (count - 1), [1] * (count - 1)
    while spare > 0:
        free = [i for i in range(count - 1) if holding[i] < most]
        mass, left = sum([portions[i] for i in free]), spare
        for i in free:
            more = min(most - holding[i], max(1, left * portions[i] // mass), spare)
            holding[i] = holding[i] + more
            spare = spare - more
    return np.array([most] + holding)


def ragged_sizes(stream_key, number_of, total, most, slope):
    if number_of == 2:
        one = jax.random.randint(stream_key, (), max(1, total - most), min(most, total - 1) + 1)
        return jnp.stack([one, total - one])
    lengths = jnp.asarray(profile(number_of, total, most, slope), jnp.int32)
    couples = (number_of - 1) // 2
    source_of, taker = lengths[1:1 + 2 * couples:2], lengths[2:2 + 2 * couples:2]
    room = jnp.minimum(source_of - 1, most - taker)
    passed = jax.random.randint(jax.random.fold_in(stream_key, 1), (couples,), 0, 1 << 20) % (room + 1)
    lengths = lengths.at[1:1 + 2 * couples:2].set(source_of - passed).at[2:2 + 2 * couples:2].set(taker + passed)
    return lengths[jax.random.permutation(jax.random.fold_in(stream_key, 2), number_of)]


def noise(rng, shape, spread, bound, cuts=(), held_as=jnp.bfloat16):
    result = spread * jax.random.normal(rng, shape, jnp.float32)
    if cuts:
        result = result * levels(rng, shape, cuts, -0.22, 0.18)
    return jnp.clip(result, -bound, bound).astype(held_as)


def setup_inputs(seed: int = 0) -> dict:
    splits = jax.random.split(jax.random.key(seed), 6)
    return {
        "window": noise(splits[0], (CHANNELS, WINDOW), 1.0, 6.0, ((0, 4), (1, 8))),
        "library": noise(splits[1], (LIBRARY, CHANNELS, TMPL_LEN), 1.0, 6.0, ((1, 4),)),
        "library_index": set_ends(jax.random.randint(splits[2], (TEMPLATES,), 0, LIBRARY), jax.random.fold_in(splits[2], 1), 0, LIBRARY - 1).astype(jnp.int32),
        "moveout": draw_moveout(jax.random.fold_in(splits[5], 71), 0),
        "group_of": jnp.searchsorted(jnp.cumsum(ragged_sizes(splits[4], GROUPS, CHANNELS, GROUP_MOST, 1)), jnp.arange(CHANNELS), side="right").astype(jnp.int32),
    }


eps = 1e-06

def normalized_templates(library, library_index):
    chosen = jnp.take(library, library_index, axis=0).astype(jnp.float32)
    centered = chosen - lax.optimization_barrier(jnp.mean(chosen, axis=-1, keepdims=True))
    factor = lax.rsqrt(lax.optimization_barrier(jnp.mean(centered * centered, axis=-1, keepdims=True)) + eps)
    return (centered * factor).astype(jnp.bfloat16)

def inverse_from_running(running):
    padded = jnp.concatenate([jnp.zeros((running.shape[0], 1), running.dtype), running], axis=1)
    mean_square = (padded[:, TMPL_LEN:] - padded[:, :-TMPL_LEN]) / TMPL_LEN
    return 1.0 / (TMPL_LEN * jnp.sqrt(mean_square + eps))

def reference(window, library, library_index, moveout, group_of):
    normalized = normalized_templates(library, library_index)
    values = window.astype(jnp.float32)
    inverse = inverse_from_running(jnp.cumsum(values * values, axis=1))
    data_freq = jnp.fft.rfft(values, axis=1)
    positions = WINDOW - TMPL_LEN + 1
    members = (group_of[:, None] == jnp.arange(GROUPS, dtype=jnp.int32)[None, :]).astype(jnp.float32)
    counts = lax.optimization_barrier(jnp.sum(members, axis=0))
    member_split = members.reshape(N_STA, CHANNELS // N_STA, GROUPS)

    def one_template(inputs):
        taps, shifts = inputs
        padded = jnp.zeros((CHANNELS, WINDOW), jnp.float32).at[:, :TMPL_LEN].set(taps.astype(jnp.float32))
        spectrum = jnp.conj(jnp.fft.rfft(padded, axis=1)) * data_freq
        full = jnp.fft.irfft(spectrum, n=WINDOW, axis=1)[:, :positions]
        weighted = full * inverse
        shifted = jax.vmap(lambda row, start: lax.dynamic_slice_in_dim(row, start, LAG_COUNT))(weighted, shifts)
        split = shifted.reshape(N_STA, CHANNELS // N_STA, LAG_COUNT)
        partial_value = jnp.einsum('scl,scg->sgl', split, member_split, precision=lax.Precision.HIGHEST)
        rounded = lax.optimization_barrier(partial_value.astype(jnp.bfloat16))
        return lax.optimization_barrier(jnp.sum(rounded.astype(jnp.float32), axis=0))
    group_sum = lax.map(one_template, (normalized, moveout))
    scale = jnp.sqrt(TMPL_LEN / counts)
    return (group_sum * scale[None, :, None]).astype(jnp.bfloat16)
```

```python
import functools

import jax
import jax.numpy as jnp
from jax import lax
from jax.experimental import pallas as pl
from jax.experimental.pallas import tpu as pltpu
from jax.sharding import PartitionSpec as P

MAX_SHIFT = 212
GROUPS = 16
EPS = 1e-06
LANES = 128
STEP = 32
SUB = LANES // STEP
SPAN = 4
MESH = pl.DeviceIdType.MESH
F32 = jnp.float32
BF16 = jnp.bfloat16


def iota(shape, dim):
    return lax.broadcasted_iota(jnp.int32, shape, dim)


def split(values):
    upper = values.astype(BF16)
    return upper, (values - upper.astype(F32)).astype(BF16)


def dot(a, b):
    return jnp.dot(a, b, preferred_element_type=F32)


def kernel(
    n_tmpl, n_sta, chans, length, rows, depth,
    win_ref, lib_ref, index_ref, move_ref, group_ref, out_ref,
    lib, gathered, counts, samples, taps, bands, aligned, power, corr, partial, arrived, row_ref,
    lib_sem, win_send, win_recv, count_send, count_recv, part_send, part_recv,
):
    mine, station = lax.axis_index("tmpl"), lax.axis_index("sta")
    eights = rows // 8
    owned = out_ref.shape[2] // LANES
    blocks = owned * n_sta

    lib_copy = pltpu.make_async_copy(lib_ref, lib, lib_sem)
    lib_copy.start()

    barrier = pltpu.get_barrier_semaphore()
    for d in range(1, n_tmpl):
        peer = lax.rem(mine + d, n_tmpl)
        pl.semaphore_signal(barrier, inc=1, device_id=(peer, station), device_id_type=MESH)
    for d in range(1, n_sta):
        peer = lax.rem(station + d, n_sta)
        pl.semaphore_signal(barrier, inc=1, device_id=(mine, peer), device_id_type=MESH)

    row_ref[...] = jnp.full(row_ref.shape, -1, jnp.int32)
    row_ref[0:1, 0:chans] = group_ref[...]
    row_ref[1:2, 0:chans] = move_ref[...]
    members = jnp.where(iota((GROUPS, LANES), 0) == row_ref[0:1, :], 1.0, 0.0)
    counts[station] = jnp.broadcast_to(jnp.sum(members, axis=1, keepdims=True), (GROUPS, LANES))

    pl.semaphore_wait(barrier, n_tmpl + n_sta - 2)

    def win_copy(d):
        return pltpu.make_async_remote_copy(
            src_ref=win_ref,
            dst_ref=gathered.at[mine],
            send_sem=win_send.at[d],
            recv_sem=win_recv.at[d],
            device_id=(lax.rem(mine + d, n_tmpl), station),
            device_id_type=MESH,
        )

    def win_arrival(d):
        return pltpu.make_async_remote_copy(
            src_ref=win_ref,
            dst_ref=gathered.at[lax.rem(mine - d + n_tmpl, n_tmpl)],
            send_sem=win_send.at[d],
            recv_sem=win_recv.at[d],
            device_id=(lax.rem(mine + d, n_tmpl), station),
            device_id_type=MESH,
        )

    def count_copy(d, slot):
        return pltpu.make_async_remote_copy(
            src_ref=counts.at[station],
            dst_ref=counts.at[slot],
            send_sem=count_send.at[d],
            recv_sem=count_recv.at[d],
            device_id=(mine, lax.rem(station + d, n_sta)),
            device_id_type=MESH,
        )

    def part_copy(d, slot):
        owner = lax.rem(station + d, n_sta)
        return pltpu.make_async_remote_copy(
            src_ref=partial.at[pl.ds(owner * owned, owned)],
            dst_ref=arrived.at[slot],
            send_sem=part_send.at[d],
            recv_sem=part_recv.at[d],
            device_id=(mine, owner),
            device_id_type=MESH,
        )

    for d in range(1, n_tmpl):
        win_copy(d).start()
    for d in range(1, n_sta):
        count_copy(d, station).start()
    gathered[mine] = win_ref[...]

    lane = iota((rows, LANES), 1)
    sub = iota((rows, LANES), 0)
    moved = jnp.sum(
        jnp.where(lane == sub, row_ref[1:2, :], 0).astype(F32), axis=1, keepdims=True
    ).astype(jnp.int32)
    moved = jnp.broadcast_to(moved, (rows, LANES))
    real = sub < chans
    far = moved >= LANES
    rest = moved & (LANES - 1)
    turn = (lane + rest) & (LANES - 1)
    inside = lane < LANES - rest
    offset = iota((4 * LANES, LANES), 0) - iota((4 * LANES, LANES), 1)
    window_band = jnp.where((offset >= 0) & (offset < length), 1.0, 0.0).astype(BF16)
    fold = jnp.where(
        (iota((8 * STEP, LANES), 0) >> 3) == (iota((8 * STEP, LANES), 1) & (STEP - 1)), 1.0, 0.0
    ).astype(BF16)
    same = (iota((SPAN * SUB * 8, 8 * STEP), 0) & 7) == (iota((SPAN * SUB * 8, 8 * STEP), 1) & 7)
    members_b = members.astype(BF16)[:, :rows]

    taps[...] = jnp.zeros(taps.shape, F32)
    lib_copy.wait()
    taps[0:chans, 0:length] = lib[index_ref[0]].astype(F32)
    chosen = taps[...]
    in_taps = iota((rows, depth), 1) < length
    centered = chosen - jnp.sum(chosen, axis=1, keepdims=True) / length
    centered = jnp.where(in_taps, centered, 0.0)
    factor = lax.rsqrt(jnp.sum(centered * centered, axis=1, keepdims=True) / length + EPS)
    normalized = (centered * factor).astype(BF16).astype(F32)
    for i in range(0, STEP, 2):
        first = normalized if i == 0 else pltpu.roll(normalized, i, 1)
        second = pltpu.roll(normalized, i + 1, 1)
        pair = jnp.concatenate(
            [first.reshape(eights, 8, depth), second.reshape(eights, 8, depth)], axis=1
        )
        bands[:, 8 * i : 8 * i + 16, :] = pair.astype(BF16)

    for d in range(1, n_tmpl):
        win_arrival(d).wait_recv()

    whole = SPAN + 4

    def chunk(step):
        base = step * SPAN
        raw = []
        for b in range(whole):
            samples[b, 0:chans, :] = gathered[base + b].astype(F32)
        for b in range(whole):
            raw.append(jnp.where(real, samples[b], 0.0))
        zero = jnp.zeros((rows, LANES), F32)
        raw.append(zero)
        turned = []
        for b in range(whole):
            value = jnp.where(far, raw[b + 1], raw[b])
            turned.append(jnp.take_along_axis(value, turn, axis=1))
        start = [jnp.where(inside, turned[b], turned[b + 1]) for b in range(whole - 1)]
        for b in range(SPAN + 2):
            views = [start[b]]
            for q in range(1, SUB):
                back = LANES - STEP * q
                views.append(
                    jnp.where(
                        lane < back,
                        pltpu.roll(start[b], back, 1),
                        pltpu.roll(start[b + 1], back, 1),
                    )
                )
            stacked = jnp.concatenate([v.reshape(eights, 8, LANES) for v in views], axis=1)
            aligned[b] = stacked.astype(BF16)
        for b in range(whole - 1):
            upper, lower = split(start[b] * start[b])
            power[0, b] = upper
            power[1, b] = lower
        inverse = []
        for p in range(SPAN):
            total = 0.0
            for half in range(2):
                left = jnp.concatenate([power[half, p + a] for a in range(4)], axis=1)
                total = total + dot(left, window_band)
            inverse.append(lax.rsqrt(total / length + EPS) / length)
        quarter = iota((SPAN, 8, LANES), 2) // STEP
        for e in range(eights):
            left = jnp.concatenate(
                [aligned[a : a + SPAN, e].reshape(SPAN * SUB * 8, LANES) for a in range(depth // LANES)],
                axis=1,
            )
            crossed = lax.dot_general(
                left, bands[e], (((1,), (1,)), ((), ())), preferred_element_type=F32
            )
            upper, lower = split(jnp.where(same, crossed, 0.0))
            folded = (dot(upper, fold) + dot(lower, fold)).reshape(SPAN, SUB, 8, LANES)
            picked = folded[:, 0]
            for q in range(1, SUB):
                picked = jnp.where(quarter == q, folded[:, q], picked)
            corr[:, 8 * e : 8 * e + 8, :] = picked
        for p in range(SPAN):
            upper, lower = split(corr[p] * inverse[p])
            partial[base + p] = (dot(members_b, upper) + dot(members_b, lower)).astype(BF16)

    if blocks == SPAN:
        chunk(0)
    else:

        @pl.loop(0, blocks // SPAN)
        def _(step):
            chunk(step)

    for d in range(1, n_sta):
        part_copy(d, station).start()
    for d in range(1, n_sta):
        count_copy(d, lax.rem(station - d + n_sta, n_sta)).wait_recv()
    total_count = counts[0]
    for s in range(1, n_sta):
        total_count = total_count + counts[s]
    scale = jnp.sqrt(length / total_count)
    arrived[station] = partial[pl.ds(station * owned, owned)]
    for d in range(1, n_sta):
        part_copy(d, lax.rem(station - d + n_sta, n_sta)).wait_recv()
    for b in range(owned):
        total = arrived[0, b].astype(F32)
        for s in range(1, n_sta):
            total = total + arrived[s, b].astype(F32)
        out_ref[0, :, LANES * b : LANES * b + LANES] = (total * scale).astype(BF16)

    for d in range(1, n_tmpl):
        win_copy(d).wait_send()
    for d in range(1, n_sta):
        count_copy(d, station).wait_send()
        part_copy(d, station).wait_send()


def on_device(n_tmpl, n_sta, window, library, library_index, moveout, group_of):
    chans, width = window.shape
    length = library.shape[2]
    lags = width * n_tmpl - length - MAX_SHIFT
    owned = lags // n_sta
    blocks = lags // LANES
    rows = -(-chans // 8) * 8
    depth = -(-(length + STEP - 1) // LANES) * LANES
    vmem = pl.BlockSpec(memory_space=pltpu.VMEM)
    return pl.pallas_call(
        functools.partial(kernel, n_tmpl, n_sta, chans, length, rows, depth),
        out_shape=jax.ShapeDtypeStruct((1, GROUPS, owned), BF16),
        in_specs=[
            vmem,
            pl.BlockSpec(memory_space=pl.ANY),
            pl.BlockSpec(memory_space=pltpu.SMEM),
            vmem,
            vmem,
        ],
        out_specs=vmem,
        scratch_shapes=[
            pltpu.VMEM(library.shape, BF16),
            pltpu.VMEM((n_tmpl, chans, width), BF16),
            pltpu.VMEM((n_sta, GROUPS, LANES), F32),
            pltpu.VMEM((SPAN + 4, rows, LANES), F32),
            pltpu.VMEM((rows, depth), F32),
            pltpu.VMEM((rows // 8, 8 * STEP, depth), BF16),
            pltpu.VMEM((SPAN + 2, rows // 8, 8 * SUB, LANES), BF16),
            pltpu.VMEM((2, SPAN + 3, rows, LANES), BF16),
            pltpu.VMEM((SPAN, rows, LANES), F32),
            pltpu.VMEM((blocks, GROUPS, LANES), BF16),
            pltpu.VMEM((n_sta, blocks // n_sta, GROUPS, LANES), BF16),
            pltpu.VMEM((8, LANES), jnp.int32),
            pltpu.SemaphoreType.DMA,
            pltpu.SemaphoreType.DMA((n_tmpl,)),
            pltpu.SemaphoreType.DMA((n_tmpl,)),
            pltpu.SemaphoreType.DMA((n_sta,)),
            pltpu.SemaphoreType.DMA((n_sta,)),
            pltpu.SemaphoreType.DMA((n_sta,)),
            pltpu.SemaphoreType.DMA((n_sta,)),
        ],
        compiler_params=pltpu.CompilerParams(
            collective_id=0, has_side_effects=True, vmem_limit_bytes=48 * 1024 * 1024
        ),
    )(window, library, library_index, moveout, group_of.reshape(1, -1))


def solution(mesh):
    in_specs = (P("sta", "tmpl"), P(None, "sta", None), P("tmpl"), P("tmpl", "sta"), P("sta"))
    body = functools.partial(on_device, mesh.shape["tmpl"], mesh.shape["sta"])
    return jax.shard_map(
        body, mesh=mesh, in_specs=in_specs, out_specs=P("tmpl", None, "sta"), check_vma=False
    )
```

```python
import functools

import jax
import jax.numpy as jnp
from jax import lax
from jax.experimental import pallas as pl
from jax.experimental.pallas import tpu as pltpu
from jax.sharding import PartitionSpec as P

MAX_SHIFT = 212
GROUPS = 16
EPS = 1e-06
LANES = 128
STEP = 32
SUB = LANES // STEP
SPAN = 4
MESH = pl.DeviceIdType.MESH
F32 = jnp.float32
BF16 = jnp.bfloat16


def iota(shape, dim):
    return lax.broadcasted_iota(jnp.int32, shape, dim)


def dot(a, b):
    return jnp.dot(a, b, preferred_element_type=F32)


def kernel(
    n_tmpl, n_sta, chans, length, rows, depth,
    win_ref, lib_ref, index_ref, move_ref, group_ref, out_ref,
    lib, moves, stations, gathered, counts, samples, taps, bands, aligned, power, corr, partial, arrived,
    row_ref, lib_sem, own_sem, move_sem, group_sem, win_send, win_recv, count_send, count_recv, part_send, part_recv,
):
    mine, station = lax.axis_index("tmpl"), lax.axis_index("sta")
    eights = rows // 8
    owned = out_ref.shape[2] // LANES
    blocks = owned * n_sta

    lib_copy = pltpu.make_async_copy(lib_ref, lib, lib_sem)
    own_copy = pltpu.make_async_copy(win_ref, gathered.at[mine], own_sem)
    move_copy = pltpu.make_async_copy(move_ref, moves, move_sem)
    group_copy = pltpu.make_async_copy(group_ref, stations, group_sem)

    barrier = pltpu.get_barrier_semaphore()
    for d in range(1, n_tmpl):
        peer = lax.rem(mine + d, n_tmpl)
        pl.semaphore_signal(barrier, inc=1, device_id=(peer, station), device_id_type=MESH)
    for d in range(1, n_sta):
        peer = lax.rem(station + d, n_sta)
        pl.semaphore_signal(barrier, inc=1, device_id=(mine, peer), device_id_type=MESH)

    for copy in (group_copy, move_copy, own_copy, lib_copy):
        copy.start()

    row_ref[...] = jnp.full(row_ref.shape, -1, jnp.int32)
    group_copy.wait()
    move_copy.wait()
    row_ref[0:1, 0:chans] = stations[...]
    row_ref[1:2, 0:chans] = moves[...]
    members = jnp.where(iota((GROUPS, LANES), 0) == row_ref[0:1, :], 1.0, 0.0)
    counts[station] = jnp.broadcast_to(jnp.sum(members, axis=1, keepdims=True), (GROUPS, LANES))

    pl.semaphore_wait(barrier, n_tmpl + n_sta - 2)

    def win_copy(d):
        return pltpu.make_async_remote_copy(
            src_ref=win_ref,
            dst_ref=gathered.at[mine],
            send_sem=win_send.at[d],
            recv_sem=win_recv.at[d],
            device_id=(lax.rem(mine + d, n_tmpl), station),
            device_id_type=MESH,
        )

    def win_arrival(d):
        return pltpu.make_async_remote_copy(
            src_ref=win_ref,
            dst_ref=gathered.at[lax.rem(mine - d + n_tmpl, n_tmpl)],
            send_sem=win_send.at[d],
            recv_sem=win_recv.at[d],
            device_id=(lax.rem(mine + d, n_tmpl), station),
            device_id_type=MESH,
        )

    def count_copy(d, slot):
        return pltpu.make_async_remote_copy(
            src_ref=counts.at[station],
            dst_ref=counts.at[slot],
            send_sem=count_send.at[d],
            recv_sem=count_recv.at[d],
            device_id=(mine, lax.rem(station + d, n_sta)),
            device_id_type=MESH,
        )

    def part_copy(d, slot):
        owner = lax.rem(station + d, n_sta)
        return pltpu.make_async_remote_copy(
            src_ref=partial.at[pl.ds(owner * owned, owned)],
            dst_ref=arrived.at[slot],
            send_sem=part_send.at[d],
            recv_sem=part_recv.at[d],
            device_id=(mine, owner),
            device_id_type=MESH,
        )

    for d in range(1, n_tmpl):
        win_copy(d).start()
    for d in range(1, n_sta):
        count_copy(d, station).start()

    lane = iota((rows, LANES), 1)
    sub = iota((rows, LANES), 0)
    moved = jnp.sum(
        jnp.where(lane == sub, row_ref[1:2, :], 0).astype(F32), axis=1, keepdims=True
    ).astype(jnp.int32)
    moved = jnp.broadcast_to(moved, (rows, LANES))
    real = sub < chans
    far = moved >= LANES
    rest = moved & (LANES - 1)
    turn = (lane + rest) & (LANES - 1)
    inside = lane < LANES - rest
    offset = iota((4 * LANES, LANES), 0) - iota((4 * LANES, LANES), 1)
    window_band = jnp.where((offset >= 0) & (offset < length), 1.0, 0.0).astype(BF16)
    row_of = iota((SPAN * SUB * 8, LANES), 0) & 7
    upper_half = row_of >= 8 // 2
    own_lane = (row_of % SUB) * STEP + (iota((SPAN * SUB * 8, LANES), 1) & (STEP - 1))
    members_b = members.astype(BF16)[:, :rows]

    which = index_ref[0]
    spot = iota((rows, 16 * chans), 1)
    take = ((spot >> 4) == iota((rows, 16 * chans), 0)) & ((spot & 15) == (which & 15))
    lib_copy.wait()
    choices = lib[:, which >> 4].reshape(16 * chans, length)
    taps[...] = jnp.zeros(taps.shape, F32)
    taps[:, 0:length] = dot(jnp.where(take, 1.0, 0.0).astype(BF16), choices)
    chosen = taps[...]
    in_taps = iota((rows, depth), 1) < length
    centered = chosen - jnp.sum(chosen, axis=1, keepdims=True) / length
    centered = jnp.where(in_taps, centered, 0.0)
    factor = lax.rsqrt(jnp.sum(centered * centered, axis=1, keepdims=True) / length + EPS)
    taps[...] = (centered * factor).astype(BF16).astype(F32)
    for c in range(rows):
        row = jnp.broadcast_to(taps[c : c + 1, :], (STEP, depth))
        band = pltpu.roll(row, 0, 1, stride=1, stride_axis=0)
        bands[c // 8, STEP * (c % 8) : STEP * (c % 8) + STEP, :] = band.astype(BF16)

    own_copy.wait()
    for d in range(1, n_tmpl):
        win_arrival(d).wait_recv()

    whole = SPAN + 4

    def chunk(step):
        base = step * SPAN
        raw = []
        for b in range(whole):
            samples[b, 0:chans, :] = gathered[base + b].astype(F32)
        for b in range(whole):
            raw.append(jnp.where(real, samples[b], 0.0))
        zero = jnp.zeros((rows, LANES), F32)
        raw.append(zero)
        turned = []
        for b in range(whole):
            value = jnp.where(far, raw[b + 1], raw[b])
            turned.append(jnp.take_along_axis(value, turn, axis=1))
        start = [jnp.where(inside, turned[b], turned[b + 1]) for b in range(whole - 1)]
        for b in range(SPAN + 2):
            views = [start[b]]
            for q in range(1, SUB):
                back = LANES - STEP * q
                views.append(
                    jnp.where(
                        lane < back,
                        pltpu.roll(start[b], back, 1),
                        pltpu.roll(start[b + 1], back, 1),
                    )
                )
            stacked = jnp.concatenate([v.reshape(eights, 8, LANES) for v in views], axis=1)
            aligned[b] = stacked.astype(BF16)
        for b in range(whole - 1):
            power[b] = (start[b] * start[b]).astype(BF16)
        left = jnp.concatenate([power[a : a + SPAN].reshape(SPAN * rows, LANES) for a in range(4)], axis=1)
        inverse = lax.rsqrt(dot(left, window_band) / length + EPS) / length
        inverse = inverse.reshape(SPAN, rows, LANES)
        quarter = iota((SPAN, 8, LANES), 2) // STEP
        for e in range(eights):
            left = jnp.concatenate(
                [aligned[a : a + SPAN, e].reshape(SPAN * SUB * 8, LANES) for a in range(depth // LANES)],
                axis=1,
            )
            crossed = lax.dot_general(
                left, bands[e], (((1,), (1,)), ((), ())), preferred_element_type=F32
            )
            half = jnp.where(upper_half, crossed[:, LANES:], crossed[:, :LANES])
            folded = jnp.take_along_axis(half, own_lane, axis=1).reshape(SPAN, SUB, 8, LANES)
            picked = folded[:, 0]
            for q in range(1, SUB):
                picked = jnp.where(quarter == q, folded[:, q], picked)
            corr[:, 8 * e : 8 * e + 8, :] = picked
        for p in range(SPAN):
            weighted = (corr[p] * inverse[p]).astype(BF16)
            partial[base + p] = dot(members_b, weighted).astype(BF16)

    if blocks == SPAN:
        chunk(0)
    else:

        @pl.loop(0, blocks // SPAN)
        def _(step):
            chunk(step)

    for d in range(1, n_sta):
        part_copy(d, station).start()
    for d in range(1, n_sta):
        count_copy(d, lax.rem(station - d + n_sta, n_sta)).wait_recv()
    total_count = counts[0]
    for s in range(1, n_sta):
        total_count = total_count + counts[s]
    scale = jnp.sqrt(length / total_count)
    arrived[station] = partial[pl.ds(station * owned, owned)]
    for d in range(1, n_sta):
        part_copy(d, lax.rem(station - d + n_sta, n_sta)).wait_recv()
    for b in range(owned):
        total = arrived[0, b].astype(F32)
        for s in range(1, n_sta):
            total = total + arrived[s, b].astype(F32)
        out_ref[0, :, LANES * b : LANES * b + LANES] = (total * scale).astype(BF16)

    for d in range(1, n_tmpl):
        win_copy(d).wait_send()
    for d in range(1, n_sta):
        count_copy(d, station).wait_send()
        part_copy(d, station).wait_send()


def on_device(n_tmpl, n_sta, window, library, library_index, moveout, group_of):
    chans, width = window.shape
    length = library.shape[2]
    lags = width * n_tmpl - length - MAX_SHIFT
    owned = lags // n_sta
    blocks = lags // LANES
    rows = -(-chans // 8) * 8
    depth = -(-(length + STEP - 1) // LANES) * LANES
    by_channel = jnp.transpose(library, (1, 0, 2)).reshape(chans, -1, 16, length)
    vmem = pl.BlockSpec(memory_space=pltpu.VMEM)
    return pl.pallas_call(
        functools.partial(kernel, n_tmpl, n_sta, chans, length, rows, depth),
        out_shape=jax.ShapeDtypeStruct((1, GROUPS, owned), BF16),
        in_specs=[
            pl.BlockSpec(memory_space=pl.ANY),
            pl.BlockSpec(memory_space=pl.ANY),
            pl.BlockSpec(memory_space=pltpu.SMEM),
            pl.BlockSpec(memory_space=pl.ANY),
            pl.BlockSpec(memory_space=pl.ANY),
        ],
        out_specs=vmem,
        scratch_shapes=[
            pltpu.VMEM(by_channel.shape, BF16),
            pltpu.VMEM((1, chans), jnp.int32),
            pltpu.VMEM((1, chans), jnp.int32),
            pltpu.VMEM((n_tmpl, chans, width), BF16),
            pltpu.VMEM((n_sta, GROUPS, LANES), F32),
            pltpu.VMEM((SPAN + 4, rows, LANES), F32),
            pltpu.VMEM((rows, depth), F32),
            pltpu.VMEM((rows // 8, 8 * STEP, depth), BF16),
            pltpu.VMEM((SPAN + 2, rows // 8, 8 * SUB, LANES), BF16),
            pltpu.VMEM((SPAN + 3, rows, LANES), BF16),
            pltpu.VMEM((SPAN, rows, LANES), F32),
            pltpu.VMEM((blocks, GROUPS, LANES), BF16),
            pltpu.VMEM((n_sta, blocks // n_sta, GROUPS, LANES), BF16),
            pltpu.VMEM((8, LANES), jnp.int32),
            pltpu.SemaphoreType.DMA,
            pltpu.SemaphoreType.DMA,
            pltpu.SemaphoreType.DMA,
            pltpu.SemaphoreType.DMA,
            pltpu.SemaphoreType.DMA((n_tmpl,)),
            pltpu.SemaphoreType.DMA((n_tmpl,)),
            pltpu.SemaphoreType.DMA((n_sta,)),
            pltpu.SemaphoreType.DMA((n_sta,)),
            pltpu.SemaphoreType.DMA((n_sta,)),
            pltpu.SemaphoreType.DMA((n_sta,)),
        ],
        compiler_params=pltpu.CompilerParams(
            collective_id=0, has_side_effects=True, vmem_limit_bytes=62 * 1024 * 1024
        ),
    )(window, by_channel, library_index, moveout, group_of.reshape(1, -1))


def solution(mesh):
    in_specs = (P("sta", "tmpl"), P(None, "sta", None), P("tmpl"), P("tmpl", "sta"), P("sta"))
    body = functools.partial(on_device, mesh.shape["tmpl"], mesh.shape["sta"])
    return jax.shard_map(
        body, mesh=mesh, in_specs=in_specs, out_specs=P("tmpl", None, "sta"), check_vma=False
    )
```

```python
import functools

import jax
import jax.numpy as jnp
from jax import lax
from jax.experimental import pallas as pl
from jax.experimental.pallas import tpu as pltpu
from jax.sharding import PartitionSpec as P

MAX_SHIFT = 212
GROUPS = 16
EPS = 1e-06
LANES = 128
STEP = 32
SUB = LANES // STEP
SPAN = 4
LIB_COPIES = 5
MESH = pl.DeviceIdType.MESH
F32 = jnp.float32
BF16 = jnp.bfloat16


def iota(shape, dim):
    return lax.broadcasted_iota(jnp.int32, shape, dim)


def dot(a, b):
    return jnp.dot(a, b, preferred_element_type=F32)


def kernel(
    n_tmpl, n_sta, chans, length, rows, depth,
    win_ref, lib_ref, index_ref, move_ref, group_ref, out_ref,
    lib, moves, stations, gathered, counts, widened, turned, taps, bands, aligned, power, corr, partial, arrived,
    row_ref, lib_sem, own_sem, move_sem, group_sem, win_send, win_recv, count_send, count_recv, part_send, part_recv,
):
    mine, station = lax.axis_index("tmpl"), lax.axis_index("sta")
    eights = rows // 8
    owned = out_ref.shape[2] // LANES
    blocks = owned * n_sta

    share = -(-chans // LIB_COPIES)
    lib_copies = []
    for k in range(LIB_COPIES):
        piece = pl.ds(k * share, min(share, chans - k * share))
        lib_copies.append(pltpu.make_async_copy(lib_ref.at[piece], lib.at[piece], lib_sem.at[k]))
    own_copy = pltpu.make_async_copy(win_ref, gathered.at[mine], own_sem)
    move_copy = pltpu.make_async_copy(move_ref, moves, move_sem)
    group_copy = pltpu.make_async_copy(group_ref, stations, group_sem)

    barrier = pltpu.get_barrier_semaphore()
    for d in range(1, n_tmpl):
        peer = lax.rem(mine + d, n_tmpl)
        pl.semaphore_signal(barrier, inc=1, device_id=(peer, station), device_id_type=MESH)
    for d in range(1, n_sta):
        peer = lax.rem(station + d, n_sta)
        pl.semaphore_signal(barrier, inc=1, device_id=(mine, peer), device_id_type=MESH)

    for copy in [group_copy, move_copy, own_copy] + lib_copies:
        copy.start()

    pl.semaphore_wait(barrier, n_tmpl + n_sta - 2)

    def win_copy(d):
        return pltpu.make_async_remote_copy(
            src_ref=win_ref,
            dst_ref=gathered.at[mine],
            send_sem=win_send.at[d],
            recv_sem=win_recv.at[d],
            device_id=(lax.rem(mine + d, n_tmpl), station),
            device_id_type=MESH,
        )

    def win_arrival(d):
        return pltpu.make_async_remote_copy(
            src_ref=win_ref,
            dst_ref=gathered.at[lax.rem(mine - d + n_tmpl, n_tmpl)],
            send_sem=win_send.at[d],
            recv_sem=win_recv.at[d],
            device_id=(lax.rem(mine + d, n_tmpl), station),
            device_id_type=MESH,
        )

    def count_copy(d, slot):
        return pltpu.make_async_remote_copy(
            src_ref=counts.at[station],
            dst_ref=counts.at[slot],
            send_sem=count_send.at[d],
            recv_sem=count_recv.at[d],
            device_id=(mine, lax.rem(station + d, n_sta)),
            device_id_type=MESH,
        )

    def part_copy(d, slot):
        owner = lax.rem(station + d, n_sta)
        return pltpu.make_async_remote_copy(
            src_ref=partial.at[pl.ds(owner * owned, owned)],
            dst_ref=arrived.at[slot],
            send_sem=part_send.at[d],
            recv_sem=part_recv.at[d],
            device_id=(mine, owner),
            device_id_type=MESH,
        )

    for d in range(1, n_tmpl):
        win_copy(d).start()
    row_ref[...] = jnp.full(row_ref.shape, -1, jnp.int32)
    group_copy.wait()
    move_copy.wait()
    row_ref[0:1, 0:chans] = stations[...]
    row_ref[1:2, 0:chans] = moves[...]
    members = jnp.where(iota((GROUPS, LANES), 0) == row_ref[0:1, :], 1.0, 0.0)
    counts[station] = jnp.broadcast_to(jnp.sum(members, axis=1, keepdims=True), (GROUPS, LANES))
    for d in range(1, n_sta):
        count_copy(d, station).start()

    lane = iota((rows, LANES), 1)
    sub = iota((rows, LANES), 0)
    moved = jnp.sum(
        jnp.where(lane == sub, row_ref[1:2, :], 0).astype(F32), axis=1, keepdims=True
    ).astype(jnp.int32)
    moved = jnp.broadcast_to(moved, (rows, LANES))
    real = sub < chans
    turns = [(lane + moved + STEP * q) & (LANES - 1) for q in range(SUB)]
    blocks_on = [(lane + moved + STEP * q) >> 7 for q in range(SUB)]
    farthest = [(LANES - 1 + MAX_SHIFT + STEP * q) >> 7 for q in range(SUB)]
    offset = iota((4 * LANES, LANES), 0) - iota((4 * LANES, LANES), 1)
    window_band = jnp.where((offset >= 0) & (offset < length), 1.0, 0.0).astype(BF16)
    row_of = iota((SPAN * SUB * 8, LANES), 0) & 7
    upper_half = row_of >= 8 // 2
    own_lane = (row_of % SUB) * STEP + (iota((SPAN * SUB * 8, LANES), 1) & (STEP - 1))
    members_b = members.astype(BF16)[:, :rows]

    which = index_ref[0]
    spot = iota((rows, 16 * chans), 1)
    take = ((spot >> 4) == iota((rows, 16 * chans), 0)) & ((spot & 15) == (which & 15))
    for copy in lib_copies:
        copy.wait()
    choices = lib[:, which >> 4].reshape(16 * chans, length)
    taps[...] = jnp.zeros(taps.shape, F32)
    taps[:, 0:length] = dot(jnp.where(take, 1.0, 0.0).astype(BF16), choices)
    chosen = taps[...]
    in_taps = iota((rows, depth), 1) < length
    centered = chosen - jnp.sum(chosen, axis=1, keepdims=True) / length
    centered = jnp.where(in_taps, centered, 0.0)
    factor = lax.rsqrt(jnp.sum(centered * centered, axis=1, keepdims=True) / length + EPS)
    taps[...] = (centered * factor).astype(BF16).astype(F32)
    for c in range(rows):
        row = jnp.broadcast_to(taps[c : c + 1, :], (STEP, depth))
        band = pltpu.roll(row, 0, 1, stride=1, stride_axis=0)
        bands[c // 8, STEP * (c % 8) : STEP * (c % 8) + STEP, :] = band.astype(BF16)

    def turn_block(slot):
        widened[0:chans, :] = gathered[slot].astype(F32)
        values = jnp.where(real, widened[...], 0.0)
        for q in range(SUB):
            turned[q, slot] = jnp.take_along_axis(values, turns[q], axis=1)

    own_copy.wait()
    turn_block(mine)
    for d in range(1, n_tmpl):
        win_arrival(d).wait_recv()
        turn_block(lax.rem(mine - d + n_tmpl, n_tmpl))

    whole = SPAN + 4

    def chunk(step):
        base = step * SPAN
        for b in range(whole - 1):
            views = []
            for q in range(SUB if b < SPAN + 2 else 1):
                value = turned[q, base + b]
                for ahead in range(1, farthest[q] + 1):
                    if b + ahead < whole:
                        value = jnp.where(blocks_on[q] == ahead, turned[q, base + b + ahead], value)
                views.append(value)
            power[b] = (views[0] * views[0]).astype(BF16)
            if b < SPAN + 2:
                stacked = jnp.concatenate([v.reshape(eights, 8, LANES) for v in views], axis=1)
                aligned[b] = stacked.astype(BF16)
        left = jnp.concatenate([power[a : a + SPAN].reshape(SPAN * rows, LANES) for a in range(4)], axis=1)
        inverse = lax.rsqrt(dot(left, window_band) / length + EPS) / length
        inverse = inverse.reshape(SPAN, rows, LANES)
        quarter = iota((SPAN, 8, LANES), 2) // STEP
        for e in range(eights):
            left = jnp.concatenate(
                [aligned[a : a + SPAN, e].reshape(SPAN * SUB * 8, LANES) for a in range(depth // LANES)],
                axis=1,
            )
            crossed = lax.dot_general(
                left, bands[e], (((1,), (1,)), ((), ())), preferred_element_type=F32
            )
            half = jnp.where(upper_half, crossed[:, LANES:], crossed[:, :LANES])
            folded = jnp.take_along_axis(half, own_lane, axis=1).reshape(SPAN, SUB, 8, LANES)
            picked = folded[:, 0]
            for q in range(1, SUB):
                picked = jnp.where(quarter == q, folded[:, q], picked)
            corr[:, 8 * e : 8 * e + 8, :] = picked
        for p in range(SPAN):
            weighted = (corr[p] * inverse[p]).astype(BF16)
            partial[base + p] = dot(members_b, weighted).astype(BF16)

    if blocks == SPAN:
        chunk(0)
    else:

        @pl.loop(0, blocks // SPAN)
        def _(step):
            chunk(step)

    for d in range(1, n_sta):
        part_copy(d, station).start()
    for d in range(1, n_sta):
        count_copy(d, lax.rem(station - d + n_sta, n_sta)).wait_recv()
    total_count = counts[0]
    for s in range(1, n_sta):
        total_count = total_count + counts[s]
    scale = jnp.sqrt(length / total_count)
    arrived[station] = partial[pl.ds(station * owned, owned)]
    for d in range(1, n_sta):
        part_copy(d, lax.rem(station - d + n_sta, n_sta)).wait_recv()
    for b in range(owned):
        total = arrived[0, b].astype(F32)
        for s in range(1, n_sta):
            total = total + arrived[s, b].astype(F32)
        out_ref[0, :, LANES * b : LANES * b + LANES] = (total * scale).astype(BF16)

    for d in range(1, n_tmpl):
        win_copy(d).wait_send()
    for d in range(1, n_sta):
        count_copy(d, station).wait_send()
        part_copy(d, station).wait_send()


def on_device(n_tmpl, n_sta, window, library, library_index, moveout, group_of):
    chans, width = window.shape
    length = library.shape[2]
    lags = width * n_tmpl - length - MAX_SHIFT
    owned = lags // n_sta
    blocks = lags // LANES
    rows = -(-chans // 8) * 8
    depth = -(-(length + STEP - 1) // LANES) * LANES
    by_channel = jnp.transpose(library, (1, 0, 2)).reshape(chans, -1, 16, length)
    vmem = pl.BlockSpec(memory_space=pltpu.VMEM)
    return pl.pallas_call(
        functools.partial(kernel, n_tmpl, n_sta, chans, length, rows, depth),
        out_shape=jax.ShapeDtypeStruct((1, GROUPS, owned), BF16),
        in_specs=[
            pl.BlockSpec(memory_space=pl.ANY),
            pl.BlockSpec(memory_space=pl.ANY),
            pl.BlockSpec(memory_space=pltpu.SMEM),
            pl.BlockSpec(memory_space=pl.ANY),
            pl.BlockSpec(memory_space=pl.ANY),
        ],
        out_specs=vmem,
        scratch_shapes=[
            pltpu.VMEM(by_channel.shape, BF16),
            pltpu.VMEM((1, chans), jnp.int32),
            pltpu.VMEM((1, chans), jnp.int32),
            pltpu.VMEM((n_tmpl, chans, width), BF16),
            pltpu.VMEM((n_sta, GROUPS, LANES), F32),
            pltpu.VMEM((rows, LANES), F32),
            pltpu.VMEM((SUB, n_tmpl, rows, LANES), F32),
            pltpu.VMEM((rows, depth), F32),
            pltpu.VMEM((rows // 8, 8 * STEP, depth), BF16),
            pltpu.VMEM((SPAN + 2, rows // 8, 8 * SUB, LANES), BF16),
            pltpu.VMEM((SPAN + 3, rows, LANES), BF16),
            pltpu.VMEM((SPAN, rows, LANES), F32),
            pltpu.VMEM((blocks, GROUPS, LANES), BF16),
            pltpu.VMEM((n_sta, blocks // n_sta, GROUPS, LANES), BF16),
            pltpu.VMEM((8, LANES), jnp.int32),
            pltpu.SemaphoreType.DMA((LIB_COPIES,)),
            pltpu.SemaphoreType.DMA,
            pltpu.SemaphoreType.DMA,
            pltpu.SemaphoreType.DMA,
            pltpu.SemaphoreType.DMA((n_tmpl,)),
            pltpu.SemaphoreType.DMA((n_tmpl,)),
            pltpu.SemaphoreType.DMA((n_sta,)),
            pltpu.SemaphoreType.DMA((n_sta,)),
            pltpu.SemaphoreType.DMA((n_sta,)),
            pltpu.SemaphoreType.DMA((n_sta,)),
        ],
        compiler_params=pltpu.CompilerParams(
            collective_id=0, has_side_effects=True, vmem_limit_bytes=56 * 1024 * 1024
        ),
    )(window, by_channel, library_index, moveout, group_of.reshape(1, -1))


def solution(mesh):
    in_specs = (P("sta", "tmpl"), P(None, "sta", None), P("tmpl"), P("tmpl", "sta"), P("sta"))
    body = functools.partial(on_device, mesh.shape["tmpl"], mesh.shape["sta"])
    return jax.shard_map(
        body, mesh=mesh, in_specs=in_specs, out_specs=P("tmpl", None, "sta"), check_vma=False
    )
```

```python
import functools

import jax
import jax.numpy as jnp
from jax import lax
from jax.experimental import pallas as pl
from jax.experimental.pallas import tpu as pltpu
from jax.sharding import PartitionSpec as P

MAX_SHIFT = 212
GROUPS = 16
EPS = 1e-06
LANES = 128
STEP = 32
SUB = LANES // STEP
SPAN = 4
LIB_COPIES = 5
MESH = pl.DeviceIdType.MESH
F32 = jnp.float32
BF16 = jnp.bfloat16


def iota(shape, dim):
    return lax.broadcasted_iota(jnp.int32, shape, dim)


def dot(a, b):
    return jnp.dot(a, b, preferred_element_type=F32)


def kernel(
    n_tmpl, n_sta, chans, length, rows, depth,
    win_ref, lib_ref, index_ref, move_ref, group_ref, out_ref,
    lib, moves, stations, gathered, counts, widened, turned, ahead_of, taps, bands, power, corr, partial, arrived,
    row_ref, lib_sem, own_sem, move_sem, group_sem, win_send, win_recv, count_send, count_recv, part_send, part_recv,
):
    mine, station = lax.axis_index("tmpl"), lax.axis_index("sta")
    eights = rows // 8
    owned = out_ref.shape[2] // LANES
    blocks = owned * n_sta

    share = -(-chans // LIB_COPIES)
    lib_copies = []
    for k in range(LIB_COPIES):
        piece = pl.ds(k * share, min(share, chans - k * share))
        lib_copies.append(pltpu.make_async_copy(lib_ref.at[piece], lib.at[piece], lib_sem.at[k]))
    own_copy = pltpu.make_async_copy(win_ref, gathered.at[mine], own_sem)
    move_copy = pltpu.make_async_copy(move_ref, moves, move_sem)
    group_copy = pltpu.make_async_copy(group_ref, stations, group_sem)

    barrier = pltpu.get_barrier_semaphore()
    for d in range(1, n_tmpl):
        peer = lax.rem(mine + d, n_tmpl)
        pl.semaphore_signal(barrier, inc=1, device_id=(peer, station), device_id_type=MESH)
    for d in range(1, n_sta):
        peer = lax.rem(station + d, n_sta)
        pl.semaphore_signal(barrier, inc=1, device_id=(mine, peer), device_id_type=MESH)

    for copy in [group_copy, move_copy, own_copy] + lib_copies:
        copy.start()

    pl.semaphore_wait(barrier, n_tmpl + n_sta - 2)

    def win_copy(d):
        return pltpu.make_async_remote_copy(
            src_ref=win_ref,
            dst_ref=gathered.at[mine],
            send_sem=win_send.at[d],
            recv_sem=win_recv.at[d],
            device_id=(lax.rem(mine + d, n_tmpl), station),
            device_id_type=MESH,
        )

    def win_arrival(d):
        return pltpu.make_async_remote_copy(
            src_ref=win_ref,
            dst_ref=gathered.at[lax.rem(mine - d + n_tmpl, n_tmpl)],
            send_sem=win_send.at[d],
            recv_sem=win_recv.at[d],
            device_id=(lax.rem(mine + d, n_tmpl), station),
            device_id_type=MESH,
        )

    def count_copy(d, slot):
        return pltpu.make_async_remote_copy(
            src_ref=counts.at[station],
            dst_ref=counts.at[slot],
            send_sem=count_send.at[d],
            recv_sem=count_recv.at[d],
            device_id=(mine, lax.rem(station + d, n_sta)),
            device_id_type=MESH,
        )

    def part_copy(d, slot):
        owner = lax.rem(station + d, n_sta)
        return pltpu.make_async_remote_copy(
            src_ref=partial.at[pl.ds(owner * owned, owned)],
            dst_ref=arrived.at[slot],
            send_sem=part_send.at[d],
            recv_sem=part_recv.at[d],
            device_id=(mine, owner),
            device_id_type=MESH,
        )

    for d in range(1, n_tmpl):
        win_copy(d).start()
    row_ref[...] = jnp.full(row_ref.shape, -1, jnp.int32)
    group_copy.wait()
    move_copy.wait()
    row_ref[0:1, 0:chans] = stations[...]
    row_ref[1:2, 0:chans] = moves[...]
    members = jnp.where(iota((GROUPS, LANES), 0) == row_ref[0:1, :], 1.0, 0.0)
    counts[station] = jnp.broadcast_to(jnp.sum(members, axis=1, keepdims=True), (GROUPS, LANES))
    for d in range(1, n_sta):
        count_copy(d, station).start()

    lane = iota((rows, LANES), 1)
    sub = iota((rows, LANES), 0)
    moved = jnp.sum(
        jnp.where(lane == sub, row_ref[1:2, :], 0).astype(F32), axis=1, keepdims=True
    ).astype(jnp.int32)
    moved = jnp.broadcast_to(moved, (rows, LANES))
    real = sub < chans
    turns = [(lane + moved + STEP * q) & (LANES - 1) for q in range(SUB)]
    for q in range(SUB):
        ahead_of[q] = ((lane + moved + STEP * q) >> 7).reshape(eights, 8, LANES)
    farthest = [(LANES - 1 + MAX_SHIFT + STEP * q) >> 7 for q in range(SUB)]
    offset = iota((4 * LANES, LANES), 0) - iota((4 * LANES, LANES), 1)
    window_band = jnp.where((offset >= 0) & (offset < length), 1.0, 0.0).astype(BF16)
    upper_half = iota((1, 8, LANES), 1) >= 8 // 2
    own_lane = (iota((1, 8, LANES), 1) % SUB) * STEP + (iota((1, 8, LANES), 2) & (STEP - 1))
    own_lane = jnp.broadcast_to(own_lane, (SPAN * SUB, 8, LANES)).reshape(SPAN * SUB * 8, LANES)
    members_b = members.astype(BF16)[:, :rows]

    which = index_ref[0]
    take = ((iota((8, LANES), 1) >> 4) == iota((8, LANES), 0)) & ((iota((8, LANES), 1) & 15) == (which & 15))
    take = jnp.where(take, 1.0, 0.0).astype(BF16)
    taps[...] = jnp.zeros(taps.shape, F32)
    lib[chans:rows] = jnp.zeros((rows - chans,) + lib.shape[1:], BF16)
    for copy in lib_copies:
        copy.wait()
    for e in range(eights):
        choices = lib[8 * e : 8 * e + 8, which >> 4].reshape(LANES, length)
        taps[e, :, 0:length] = dot(take, choices)
    chosen = taps[...].reshape(rows, depth)
    in_taps = iota((rows, depth), 1) < length
    centered = chosen - jnp.sum(chosen, axis=1, keepdims=True) / length
    centered = jnp.where(in_taps, centered, 0.0)
    factor = lax.rsqrt(jnp.sum(centered * centered, axis=1, keepdims=True) / length + EPS)
    taps[...] = (centered * factor).astype(BF16).astype(F32).reshape(eights, 8, depth)

    @pl.loop(0, eights)
    def _(e):
        for c in range(8):
            row = jnp.broadcast_to(taps[e, c : c + 1, :], (STEP, depth))
            band = pltpu.roll(row, 0, 1, stride=1, stride_axis=0)
            bands[e, STEP * c : STEP * c + STEP, :] = band.astype(BF16)

    def turn_block(slot):
        widened[0:chans, :] = gathered[slot].astype(F32)
        values = jnp.where(real, widened[...], 0.0)
        for q in range(SUB):
            turned[q, slot] = jnp.take_along_axis(values, turns[q], axis=1).reshape(eights, 8, LANES)

    own_copy.wait()
    turn_block(mine)

    @pl.loop(1, n_tmpl)
    def _(d):
        win_arrival(d).wait_recv()
        turn_block(lax.rem(mine - d + n_tmpl, n_tmpl))

    whole = SPAN + 4

    def chunk(step):
        base = step * SPAN
        quarter = iota((SPAN, 8, LANES), 2) // STEP

        @pl.loop(0, eights, unroll=2)
        def _(e):
            pieces = []
            for b in range(whole - 1):
                views = []
                for q in range(SUB if b < SPAN + 2 else 1):
                    value = turned[q, base + b, e]
                    for ahead in range(1, farthest[q] + 1):
                        if b + ahead < whole:
                            value = jnp.where(ahead_of[q, e] == ahead, turned[q, base + b + ahead, e], value)
                    views.append(value)
                power[b, e] = views[0] * views[0]
                if b < SPAN + 2:
                    pieces.append(jnp.concatenate(views, axis=0).astype(BF16))
            left = jnp.concatenate(
                [jnp.concatenate(pieces[a : a + SPAN], axis=0) for a in range(depth // LANES)], axis=1
            )
            crossed = lax.dot_general(
                left, bands[e], (((1,), (1,)), ((), ())), preferred_element_type=F32
            ).reshape(SPAN * SUB, 8, 8 * STEP)
            half = jnp.where(upper_half, crossed[:, :, LANES:], crossed[:, :, :LANES])
            folded = jnp.take_along_axis(half.reshape(SPAN * SUB * 8, LANES), own_lane, axis=1)
            folded = folded.reshape(SPAN, SUB, 8, LANES)
            picked = folded[:, 0]
            for q in range(1, SUB):
                picked = jnp.where(quarter == q, folded[:, q], picked)
            corr[:, e] = picked

        squares = [power[b].reshape(rows, LANES).astype(BF16) for b in range(whole - 1)]
        left = jnp.concatenate(
            [jnp.concatenate(squares[a : a + SPAN], axis=0) for a in range(4)], axis=1
        )
        inverse = lax.rsqrt(dot(left, window_band) / length + EPS) / length
        inverse = inverse.reshape(SPAN, rows, LANES)
        for p in range(SPAN):
            weighted = (corr[p].reshape(rows, LANES) * inverse[p]).astype(BF16)
            partial[base + p] = dot(members_b, weighted).astype(BF16)

    if blocks == SPAN:
        chunk(0)
    else:

        @pl.loop(0, blocks // SPAN)
        def _(step):
            chunk(step)

    for d in range(1, n_sta):
        part_copy(d, station).start()
    for d in range(1, n_sta):
        count_copy(d, lax.rem(station - d + n_sta, n_sta)).wait_recv()
    total_count = counts[0]
    for s in range(1, n_sta):
        total_count = total_count + counts[s]
    scale = jnp.sqrt(length / total_count)
    arrived[station] = partial[pl.ds(station * owned, owned)]
    for d in range(1, n_sta):
        part_copy(d, lax.rem(station - d + n_sta, n_sta)).wait_recv()
    for b in range(owned):
        total = arrived[0, b].astype(F32)
        for s in range(1, n_sta):
            total = total + arrived[s, b].astype(F32)
        out_ref[0, :, LANES * b : LANES * b + LANES] = (total * scale).astype(BF16)

    for d in range(1, n_tmpl):
        win_copy(d).wait_send()
    for d in range(1, n_sta):
        count_copy(d, station).wait_send()
        part_copy(d, station).wait_send()


def on_device(n_tmpl, n_sta, window, library, library_index, moveout, group_of):
    chans, width = window.shape
    length = library.shape[2]
    lags = width * n_tmpl - length - MAX_SHIFT
    owned = lags // n_sta
    blocks = lags // LANES
    rows = -(-chans // 8) * 8
    depth = -(-(length + STEP - 1) // LANES) * LANES
    by_channel = jnp.transpose(library, (1, 0, 2)).reshape(chans, -1, 16, length)
    vmem = pl.BlockSpec(memory_space=pltpu.VMEM)
    return pl.pallas_call(
        functools.partial(kernel, n_tmpl, n_sta, chans, length, rows, depth),
        out_shape=pltpu.VMEM((1, GROUPS, owned), BF16),
        in_specs=[
            pl.BlockSpec(memory_space=pltpu.HBM),
            pl.BlockSpec(memory_space=pltpu.HBM),
            pl.BlockSpec(memory_space=pltpu.SMEM),
            pl.BlockSpec(memory_space=pltpu.HBM),
            pl.BlockSpec(memory_space=pltpu.HBM),
        ],
        out_specs=vmem,
        scratch_shapes=[
            pltpu.VMEM((rows,) + by_channel.shape[1:], BF16),
            pltpu.VMEM((1, chans), jnp.int32),
            pltpu.VMEM((1, chans), jnp.int32),
            pltpu.VMEM((n_tmpl, chans, width), BF16),
            pltpu.VMEM((n_sta, GROUPS, LANES), F32),
            pltpu.VMEM((rows, LANES), F32),
            pltpu.VMEM((SUB, n_tmpl, rows // 8, 8, LANES), F32),
            pltpu.VMEM((SUB, rows // 8, 8, LANES), jnp.int32),
            pltpu.VMEM((rows // 8, 8, depth), F32),
            pltpu.VMEM((rows // 8, 8 * STEP, depth), BF16),
            pltpu.VMEM((SPAN + 3, rows // 8, 8, LANES), F32),
            pltpu.VMEM((SPAN, rows // 8, 8, LANES), F32),
            pltpu.VMEM((blocks, GROUPS, LANES), BF16),
            pltpu.VMEM((n_sta, blocks // n_sta, GROUPS, LANES), BF16),
            pltpu.VMEM((8, LANES), jnp.int32),
            pltpu.SemaphoreType.DMA((LIB_COPIES,)),
            pltpu.SemaphoreType.DMA,
            pltpu.SemaphoreType.DMA,
            pltpu.SemaphoreType.DMA,
            pltpu.SemaphoreType.DMA((n_tmpl,)),
            pltpu.SemaphoreType.DMA((n_tmpl,)),
            pltpu.SemaphoreType.DMA((n_sta,)),
            pltpu.SemaphoreType.DMA((n_sta,)),
            pltpu.SemaphoreType.DMA((n_sta,)),
            pltpu.SemaphoreType.DMA((n_sta,)),
        ],
        compiler_params=pltpu.CompilerParams(
            collective_id=0, has_side_effects=True, vmem_limit_bytes=52 * 1024 * 1024
        ),
    )(window, by_channel, library_index, moveout, group_of.reshape(1, -1))


def solution(mesh):
    in_specs = (P("sta", "tmpl"), P(None, "sta", None), P("tmpl"), P("tmpl", "sta"), P("sta"))
    body = functools.partial(on_device, mesh.shape["tmpl"], mesh.shape["sta"])
    return jax.shard_map(
        body, mesh=mesh, in_specs=in_specs, out_specs=P("tmpl", None, "sta"), check_vma=False
    )
```

```python
import functools

import jax
import jax.numpy as jnp
from jax import lax
from jax.experimental import pallas as pl
from jax.experimental.pallas import tpu as pltpu
from jax.sharding import PartitionSpec as P

MAX_SHIFT = 212
GROUPS = 16
EPS = 1e-06
LANES = 128
STEP = 32
SUB = LANES // STEP
SPAN = 4
MESH = pl.DeviceIdType.MESH
F32 = jnp.float32
BF16 = jnp.bfloat16


def iota(shape, dim):
    return lax.broadcasted_iota(jnp.int32, shape, dim)


def dot(a, b):
    return jnp.dot(a, b, preferred_element_type=F32)


def kernel(
    n_tmpl, n_sta, chans, length, rows, depth,
    win_ref, lib_ref, index_ref, move_ref, group_ref, out_ref,
    lib, moves, stations, gathered, counts, samples, taps, bands, aligned, power, corr, partial, arrived,
    row_ref, lib_sem, own_sem, move_sem, group_sem, win_send, win_recv, count_send, count_recv, part_send, part_recv,
):
    mine, station = lax.axis_index("tmpl"), lax.axis_index("sta")
    eights = rows // 8
    owned = out_ref.shape[2] // LANES
    blocks = owned * n_sta

    lib_copy = pltpu.make_async_copy(lib_ref, lib.at[pl.ds(0, chans)], lib_sem)
    own_copy = pltpu.make_async_copy(win_ref, gathered.at[mine], own_sem)
    move_copy = pltpu.make_async_copy(move_ref, moves, move_sem)
    group_copy = pltpu.make_async_copy(group_ref, stations, group_sem)

    barrier = pltpu.get_barrier_semaphore()
    for d in range(1, n_tmpl):
        peer = lax.rem(mine + d, n_tmpl)
        pl.semaphore_signal(barrier, inc=1, device_id=(peer, station), device_id_type=MESH)
    for d in range(1, n_sta):
        peer = lax.rem(station + d, n_sta)
        pl.semaphore_signal(barrier, inc=1, device_id=(mine, peer), device_id_type=MESH)

    for copy in (group_copy, move_copy, own_copy, lib_copy):
        copy.start()

    pl.semaphore_wait(barrier, n_tmpl + n_sta - 2)

    def win_copy(d):
        return pltpu.make_async_remote_copy(
            src_ref=win_ref,
            dst_ref=gathered.at[mine],
            send_sem=win_send.at[d],
            recv_sem=win_recv.at[d],
            device_id=(lax.rem(mine + d, n_tmpl), station),
            device_id_type=MESH,
        )

    def win_arrival(d):
        return pltpu.make_async_remote_copy(
            src_ref=win_ref,
            dst_ref=gathered.at[lax.rem(mine - d + n_tmpl, n_tmpl)],
            send_sem=win_send.at[d],
            recv_sem=win_recv.at[d],
            device_id=(lax.rem(mine + d, n_tmpl), station),
            device_id_type=MESH,
        )

    def count_copy(d, slot):
        return pltpu.make_async_remote_copy(
            src_ref=counts.at[station],
            dst_ref=counts.at[slot],
            send_sem=count_send.at[d],
            recv_sem=count_recv.at[d],
            device_id=(mine, lax.rem(station + d, n_sta)),
            device_id_type=MESH,
        )

    def part_copy(d, slot):
        owner = lax.rem(station + d, n_sta)
        return pltpu.make_async_remote_copy(
            src_ref=partial.at[pl.ds(owner * owned, owned)],
            dst_ref=arrived.at[slot],
            send_sem=part_send.at[d],
            recv_sem=part_recv.at[d],
            device_id=(mine, owner),
            device_id_type=MESH,
        )

    for d in range(1, n_tmpl):
        win_copy(d).start()
    row_ref[...] = jnp.full(row_ref.shape, -1, jnp.int32)
    group_copy.wait()
    move_copy.wait()
    row_ref[0:1, 0:chans] = stations[...]
    row_ref[1:2, 0:chans] = moves[...]
    members = jnp.where(iota((GROUPS, LANES), 0) == row_ref[0:1, :], 1.0, 0.0)
    counts[station] = jnp.broadcast_to(jnp.sum(members, axis=1, keepdims=True), (GROUPS, LANES))
    for d in range(1, n_sta):
        count_copy(d, station).start()

    lane = iota((rows, LANES), 1)
    sub = iota((rows, LANES), 0)
    moved = jnp.sum(
        jnp.where(lane == sub, row_ref[1:2, :], 0).astype(F32), axis=1, keepdims=True
    ).astype(jnp.int32)
    moved = jnp.broadcast_to(moved, (rows, LANES))
    real = sub < chans
    far = moved >= LANES
    rest = moved & (LANES - 1)
    turn = (lane + rest) & (LANES - 1)
    inside = lane < LANES - rest
    offset = iota((4 * LANES, LANES), 0) - iota((4 * LANES, LANES), 1)
    window_band = jnp.where((offset >= 0) & (offset < length), 1.0, 0.0).astype(BF16)
    own = iota((8, LANES), 0)
    upper_half = own >= 8 // 2
    own = own % SUB
    quarter = iota((8, LANES), 1) // STEP
    members_b = members.astype(BF16)[:, :rows]

    which = index_ref[0]
    take = ((iota((8, LANES), 1) >> 4) == iota((8, LANES), 0)) & ((iota((8, LANES), 1) & 15) == (which & 15))
    take = jnp.where(take, 1.0, 0.0).astype(BF16)
    taps[...] = jnp.zeros(taps.shape, F32)
    lib[chans:rows] = jnp.zeros((rows - chans,) + lib.shape[1:], BF16)
    lib_copy.wait()
    for e in range(eights):
        choices = lib[8 * e : 8 * e + 8, which >> 4].reshape(LANES, length)
        taps[8 * e : 8 * e + 8, 0:length] = dot(take, choices)
    chosen = taps[...]
    in_taps = iota((rows, depth), 1) < length
    centered = chosen - jnp.sum(chosen, axis=1, keepdims=True) / length
    centered = jnp.where(in_taps, centered, 0.0)
    factor = lax.rsqrt(jnp.sum(centered * centered, axis=1, keepdims=True) / length + EPS)
    taps[...] = (centered * factor).astype(BF16).astype(F32)
    for c in range(rows):
        row = jnp.broadcast_to(taps[c : c + 1, :], (STEP, depth))
        band = pltpu.roll(row, 0, 1, stride=1, stride_axis=0)
        bands[c // 8, STEP * (c % 8) : STEP * (c % 8) + STEP, :] = band.astype(BF16)

    own_copy.wait()
    for d in range(1, n_tmpl):
        win_arrival(d).wait_recv()

    whole = SPAN + 4

    def chunk(step):
        base = step * SPAN
        raw = []
        for b in range(whole):
            samples[b, 0:chans, :] = gathered[base + b].astype(F32)
        for b in range(whole):
            raw.append(jnp.where(real, samples[b], 0.0))
        zero = jnp.zeros((rows, LANES), F32)
        raw.append(zero)
        turned = []
        for b in range(whole):
            value = jnp.where(far, raw[b + 1], raw[b])
            turned.append(jnp.take_along_axis(value, turn, axis=1))
        start = [jnp.where(inside, turned[b], turned[b + 1]) for b in range(whole - 1)]
        rolled = [
            [start[b]] + [pltpu.roll(start[b], LANES - STEP * q, 1) for q in range(1, SUB)]
            for b in range(whole - 1)
        ]
        for b in range(SPAN + 2):
            views = [start[b]]
            for q in range(1, SUB):
                views.append(jnp.where(lane < LANES - STEP * q, rolled[b][q], rolled[b + 1][q]))
            stacked = jnp.concatenate([v.reshape(eights, 8, LANES) for v in views], axis=1)
            aligned[b] = stacked.astype(BF16)
        for b in range(whole - 1):
            power[b] = (start[b] * start[b]).astype(BF16)
        left = jnp.concatenate([power[a : a + SPAN].reshape(SPAN * rows, LANES) for a in range(4)], axis=1)
        inverse = lax.rsqrt(dot(left, window_band) / length + EPS) / length
        inverse = inverse.reshape(SPAN, rows, LANES)
        for e in range(eights):
            left = jnp.concatenate(
                [aligned[a : a + SPAN, e].reshape(SPAN * SUB * 8, LANES) for a in range(depth // LANES)],
                axis=1,
            )
            crossed = lax.dot_general(
                left, bands[e], (((1,), (1,)), ((), ())), preferred_element_type=F32
            )
            for p in range(SPAN):
                halves = []
                for q in range(SUB):
                    at = (p * SUB + q) * 8
                    halves.append(
                        jnp.where(upper_half, crossed[at : at + 8, LANES:], crossed[at : at + 8, :LANES])
                    )
                for r in range(SUB):
                    value = halves[r]
                    for c in range(1, SUB):
                        value = jnp.where(own == c, halves[(r + c) % SUB], value)
                    if r == 0:
                        picked = value
                    else:
                        value = pltpu.roll(value, STEP * r, 1)
                        picked = jnp.where(quarter == (own + r) % SUB, value, picked)
                corr[p, 8 * e : 8 * e + 8, :] = picked
        for p in range(SPAN):
            weighted = (corr[p] * inverse[p]).astype(BF16)
            partial[base + p] = dot(members_b, weighted).astype(BF16)

    if blocks == SPAN:
        chunk(0)
    else:

        @pl.loop(0, blocks // SPAN)
        def _(step):
            chunk(step)

    for d in range(1, n_sta):
        part_copy(d, station).start()
    for d in range(1, n_sta):
        count_copy(d, lax.rem(station - d + n_sta, n_sta)).wait_recv()
    total_count = counts[0]
    for s in range(1, n_sta):
        total_count = total_count + counts[s]
    scale = jnp.sqrt(length / total_count)
    arrived[station] = partial[pl.ds(station * owned, owned)]
    for d in range(1, n_sta):
        part_copy(d, lax.rem(station - d + n_sta, n_sta)).wait_recv()
    for b in range(owned):
        total = arrived[0, b].astype(F32)
        for s in range(1, n_sta):
            total = total + arrived[s, b].astype(F32)
        out_ref[0, :, LANES * b : LANES * b + LANES] = (total * scale).astype(BF16)

    for d in range(1, n_tmpl):
        win_copy(d).wait_send()
    for d in range(1, n_sta):
        count_copy(d, station).wait_send()
        part_copy(d, station).wait_send()


def on_device(n_tmpl, n_sta, window, library, library_index, moveout, group_of):
    chans, width = window.shape
    length = library.shape[2]
    lags = width * n_tmpl - length - MAX_SHIFT
    owned = lags // n_sta
    blocks = lags // LANES
    rows = -(-chans // 8) * 8
    depth = -(-(length + STEP - 1) // LANES) * LANES
    by_channel = jnp.transpose(library, (1, 0, 2)).reshape(chans, -1, 16, length)
    vmem = pl.BlockSpec(memory_space=pltpu.VMEM)
    return pl.pallas_call(
        functools.partial(kernel, n_tmpl, n_sta, chans, length, rows, depth),
        out_shape=pltpu.VMEM((1, GROUPS, owned), BF16),
        in_specs=[
            pl.BlockSpec(memory_space=pl.ANY),
            pl.BlockSpec(memory_space=pl.ANY),
            pl.BlockSpec(memory_space=pltpu.SMEM),
            pl.BlockSpec(memory_space=pl.ANY),
            pl.BlockSpec(memory_space=pl.ANY),
        ],
        out_specs=vmem,
        scratch_shapes=[
            pltpu.VMEM((rows,) + by_channel.shape[1:], BF16),
            pltpu.VMEM((1, chans), jnp.int32),
            pltpu.VMEM((1, chans), jnp.int32),
            pltpu.VMEM((n_tmpl, chans, width), BF16),
            pltpu.VMEM((n_sta, GROUPS, LANES), F32),
            pltpu.VMEM((SPAN + 4, rows, LANES), F32),
            pltpu.VMEM((rows, depth), F32),
            pltpu.VMEM((rows // 8, 8 * STEP, depth), BF16),
            pltpu.VMEM((SPAN + 2, rows // 8, 8 * SUB, LANES), BF16),
            pltpu.VMEM((SPAN + 3, rows, LANES), BF16),
            pltpu.VMEM((SPAN, rows, LANES), F32),
            pltpu.VMEM((blocks, GROUPS, LANES), BF16),
            pltpu.VMEM((n_sta, blocks // n_sta, GROUPS, LANES), BF16),
            pltpu.VMEM((8, LANES), jnp.int32),
            pltpu.SemaphoreType.DMA,
            pltpu.SemaphoreType.DMA,
            pltpu.SemaphoreType.DMA,
            pltpu.SemaphoreType.DMA,
            pltpu.SemaphoreType.DMA((n_tmpl,)),
            pltpu.SemaphoreType.DMA((n_tmpl,)),
            pltpu.SemaphoreType.DMA((n_sta,)),
            pltpu.SemaphoreType.DMA((n_sta,)),
            pltpu.SemaphoreType.DMA((n_sta,)),
            pltpu.SemaphoreType.DMA((n_sta,)),
        ],
        compiler_params=pltpu.CompilerParams(
            collective_id=0, has_side_effects=True, vmem_limit_bytes=56 * 1024 * 1024
        ),
    )(window, by_channel, library_index, moveout, group_of.reshape(1, -1))


def solution(mesh):
    in_specs = (P("sta", "tmpl"), P(None, "sta", None), P("tmpl"), P("tmpl", "sta"), P("sta"))
    body = functools.partial(on_device, mesh.shape["tmpl"], mesh.shape["sta"])
    return jax.shard_map(
        body, mesh=mesh, in_specs=in_specs, out_specs=P("tmpl", None, "sta"), check_vma=False
    )
```

```python
import functools

import jax
import jax.numpy as jnp
from jax import lax
from jax.experimental import pallas as pl
from jax.experimental.pallas import tpu as pltpu
from jax.sharding import PartitionSpec as P

MAX_SHIFT = 212
GROUPS = 16
EPS = 1e-06
LANES = 128
STEP = 32
SUB = LANES // STEP
SPAN = 4
LIB_COPIES = 5
MESH = pl.DeviceIdType.MESH
F32 = jnp.float32
BF16 = jnp.bfloat16


def iota(shape, dim):
    return lax.broadcasted_iota(jnp.int32, shape, dim)


def dot(a, b):
    return jnp.dot(a, b, preferred_element_type=F32)


def kernel(
    n_tmpl, n_sta, chans, length, rows, depth,
    win_ref, lib_ref, index_ref, move_ref, group_ref, out_ref,
    lib, moves, stations, gathered, counts, samples, taps, bands, aligned, power, corr, partial, arrived,
    row_ref, lib_sem, own_sem, move_sem, group_sem, win_send, win_recv, count_send, count_recv, part_send, part_recv,
):
    mine, station = lax.axis_index("tmpl"), lax.axis_index("sta")
    eights = rows // 8
    owned = out_ref.shape[2] // LANES
    blocks = owned * n_sta

    share = -(-chans // LIB_COPIES)
    lib_copies = []
    for k in range(LIB_COPIES):
        piece = pl.ds(k * share, min(share, chans - k * share))
        lib_copies.append(pltpu.make_async_copy(lib_ref.at[piece], lib.at[piece], lib_sem.at[k]))
    own_copy = pltpu.make_async_copy(win_ref, gathered.at[mine], own_sem)
    move_copy = pltpu.make_async_copy(move_ref, moves, move_sem)
    group_copy = pltpu.make_async_copy(group_ref, stations, group_sem)

    barrier = pltpu.get_barrier_semaphore()
    for d in range(1, n_tmpl):
        peer = lax.rem(mine + d, n_tmpl)
        pl.semaphore_signal(barrier, inc=1, device_id=(peer, station), device_id_type=MESH)
    for d in range(1, n_sta):
        peer = lax.rem(station + d, n_sta)
        pl.semaphore_signal(barrier, inc=1, device_id=(mine, peer), device_id_type=MESH)

    for copy in [group_copy, move_copy, own_copy] + lib_copies:
        copy.start()

    pl.semaphore_wait(barrier, n_tmpl + n_sta - 2)

    def win_copy(d):
        return pltpu.make_async_remote_copy(
            src_ref=win_ref,
            dst_ref=gathered.at[mine],
            send_sem=win_send.at[d],
            recv_sem=win_recv.at[d],
            device_id=(lax.rem(mine + d, n_tmpl), station),
            device_id_type=MESH,
        )

    def win_arrival(d):
        return pltpu.make_async_remote_copy(
            src_ref=win_ref,
            dst_ref=gathered.at[lax.rem(mine - d + n_tmpl, n_tmpl)],
            send_sem=win_send.at[d],
            recv_sem=win_recv.at[d],
            device_id=(lax.rem(mine + d, n_tmpl), station),
            device_id_type=MESH,
        )

    def count_copy(d, slot):
        return pltpu.make_async_remote_copy(
            src_ref=counts.at[station],
            dst_ref=counts.at[slot],
            send_sem=count_send.at[d],
            recv_sem=count_recv.at[d],
            device_id=(mine, lax.rem(station + d, n_sta)),
            device_id_type=MESH,
        )

    def part_copy(d, slot):
        owner = lax.rem(station + d, n_sta)
        return pltpu.make_async_remote_copy(
            src_ref=partial.at[pl.ds(owner * owned, owned)],
            dst_ref=arrived.at[slot],
            send_sem=part_send.at[d],
            recv_sem=part_recv.at[d],
            device_id=(mine, owner),
            device_id_type=MESH,
        )

    for d in range(1, n_tmpl):
        win_copy(d).start()
    row_ref[...] = jnp.full(row_ref.shape, -1, jnp.int32)
    group_copy.wait()
    move_copy.wait()
    row_ref[0:1, 0:chans] = stations[...]
    row_ref[1:2, 0:chans] = moves[...]
    members = jnp.where(iota((GROUPS, LANES), 0) == row_ref[0:1, :], 1.0, 0.0)
    counts[station] = jnp.broadcast_to(jnp.sum(members, axis=1, keepdims=True), (GROUPS, LANES))
    for d in range(1, n_sta):
        count_copy(d, station).start()

    lane = iota((rows, LANES), 1)
    sub = iota((rows, LANES), 0)
    moved = jnp.sum(
        jnp.where(lane == sub, row_ref[1:2, :], 0).astype(F32), axis=1, keepdims=True
    ).astype(jnp.int32)
    moved = jnp.broadcast_to(moved, (rows, LANES))
    real = sub < chans
    far = moved >= LANES
    rest = moved & (LANES - 1)
    turn = (lane + rest) & (LANES - 1)
    inside = lane < LANES - rest
    offset = iota((4 * LANES, LANES), 0) - iota((4 * LANES, LANES), 1)
    window_band = jnp.where((offset >= 0) & (offset < length), 1.0, 0.0).astype(BF16)
    own = iota((8, LANES), 0)
    upper_half = own >= 8 // 2
    own = own % SUB
    quarter = iota((8, LANES), 1) // STEP
    members_b = members.astype(BF16)[:, :rows]

    which = index_ref[0]
    take = ((iota((8, LANES), 1) >> 4) == iota((8, LANES), 0)) & ((iota((8, LANES), 1) & 15) == (which & 15))
    take = jnp.where(take, 1.0, 0.0).astype(BF16)
    taps[...] = jnp.zeros(taps.shape, F32)
    lib[chans:rows] = jnp.zeros((rows - chans,) + lib.shape[1:], BF16)
    for copy in lib_copies:
        copy.wait()
    for e in range(eights):
        choices = lib[8 * e : 8 * e + 8, which >> 4].reshape(LANES, length)
        taps[8 * e : 8 * e + 8, 0:length] = dot(take, choices)
    chosen = taps[...]
    in_taps = iota((rows, depth), 1) < length
    centered = chosen - jnp.sum(chosen, axis=1, keepdims=True) / length
    centered = jnp.where(in_taps, centered, 0.0)
    factor = lax.rsqrt(jnp.sum(centered * centered, axis=1, keepdims=True) / length + EPS)
    taps[...] = (centered * factor).astype(BF16).astype(F32)
    for c in range(rows):
        row = jnp.broadcast_to(taps[c : c + 1, :], (STEP, depth))
        band = pltpu.roll(row, 0, 1, stride=1, stride_axis=0)
        bands[c // 8, STEP * (c % 8) : STEP * (c % 8) + STEP, :] = band.astype(BF16)

    own_copy.wait()
    samples[mine, 0:chans, :] = gathered[mine].astype(F32)
    for d in range(1, n_tmpl):
        win_arrival(d).wait_recv()
        slot = lax.rem(mine - d + n_tmpl, n_tmpl)
        samples[slot, 0:chans, :] = gathered[slot].astype(F32)

    whole = SPAN + 4

    def chunk(step):
        base = step * SPAN
        raw = []
        for b in range(whole):
            raw.append(jnp.where(real, samples[base + b], 0.0))
        zero = jnp.zeros((rows, LANES), F32)
        raw.append(zero)
        turned = []
        for b in range(whole):
            value = jnp.where(far, raw[b + 1], raw[b])
            turned.append(jnp.take_along_axis(value, turn, axis=1))
        start = [jnp.where(inside, turned[b], turned[b + 1]) for b in range(whole - 1)]
        rolled = [
            [start[b]] + [pltpu.roll(start[b], LANES - STEP * q, 1) for q in range(1, SUB)]
            for b in range(whole - 1)
        ]
        for b in range(SPAN + 2):
            views = [start[b]]
            for q in range(1, SUB):
                views.append(jnp.where(lane < LANES - STEP * q, rolled[b][q], rolled[b + 1][q]))
            stacked = jnp.concatenate([v.reshape(eights, 8, LANES) for v in views], axis=1)
            aligned[b] = stacked.astype(BF16)
        for b in range(whole - 1):
            power[b] = (start[b] * start[b]).astype(BF16)
        left = jnp.concatenate([power[a : a + SPAN].reshape(SPAN * rows, LANES) for a in range(4)], axis=1)
        inverse = lax.rsqrt(dot(left, window_band) / length + EPS) / length
        inverse = inverse.reshape(SPAN, rows, LANES)
        for e in range(eights):
            left = jnp.concatenate(
                [aligned[a : a + SPAN, e].reshape(SPAN * SUB * 8, LANES) for a in range(depth // LANES)],
                axis=1,
            )
            crossed = lax.dot_general(
                left, bands[e], (((1,), (1,)), ((), ())), preferred_element_type=F32
            )
            for p in range(SPAN):
                halves = []
                for q in range(SUB):
                    at = (p * SUB + q) * 8
                    halves.append(
                        jnp.where(upper_half, crossed[at : at + 8, LANES:], crossed[at : at + 8, :LANES])
                    )
                for r in range(SUB):
                    value = halves[r]
                    for c in range(1, SUB):
                        value = jnp.where(own == c, halves[(r + c) % SUB], value)
                    if r == 0:
                        picked = value
                    else:
                        value = pltpu.roll(value, STEP * r, 1)
                        picked = jnp.where(quarter == (own + r) % SUB, value, picked)
                corr[p, 8 * e : 8 * e + 8, :] = picked
        for p in range(SPAN):
            weighted = (corr[p] * inverse[p]).astype(BF16)
            partial[base + p] = dot(members_b, weighted).astype(BF16)

    if blocks == SPAN:
        chunk(0)
    else:

        @pl.loop(0, blocks // SPAN)
        def _(step):
            chunk(step)

    for d in range(1, n_sta):
        part_copy(d, station).start()
    for d in range(1, n_sta):
        count_copy(d, lax.rem(station - d + n_sta, n_sta)).wait_recv()
    total_count = counts[0]
    for s in range(1, n_sta):
        total_count = total_count + counts[s]
    scale = jnp.sqrt(length / total_count)
    arrived[station] = partial[pl.ds(station * owned, owned)]
    for d in range(1, n_sta):
        part_copy(d, lax.rem(station - d + n_sta, n_sta)).wait_recv()
    for b in range(owned):
        total = arrived[0, b].astype(F32)
        for s in range(1, n_sta):
            total = total + arrived[s, b].astype(F32)
        out_ref[0, :, LANES * b : LANES * b + LANES] = (total * scale).astype(BF16)

    for d in range(1, n_tmpl):
        win_copy(d).wait_send()
    for d in range(1, n_sta):
        count_copy(d, station).wait_send()
        part_copy(d, station).wait_send()


def on_device(n_tmpl, n_sta, window, library, library_index, moveout, group_of):
    chans, width = window.shape
    length = library.shape[2]
    lags = width * n_tmpl - length - MAX_SHIFT
    owned = lags // n_sta
    blocks = lags // LANES
    rows = -(-chans // 8) * 8
    depth = -(-(length + STEP - 1) // LANES) * LANES
    by_channel = jnp.transpose(library, (1, 0, 2)).reshape(chans, -1, 16, length)
    vmem = pl.BlockSpec(memory_space=pltpu.VMEM)
    return pl.pallas_call(
        functools.partial(kernel, n_tmpl, n_sta, chans, length, rows, depth),
        out_shape=pltpu.VMEM((1, GROUPS, owned), BF16),
        in_specs=[
            pl.BlockSpec(memory_space=pl.ANY),
            pl.BlockSpec(memory_space=pl.ANY),
            pl.BlockSpec(memory_space=pltpu.SMEM),
            pl.BlockSpec(memory_space=pl.ANY),
            pl.BlockSpec(memory_space=pl.ANY),
        ],
        out_specs=vmem,
        scratch_shapes=[
            pltpu.VMEM((rows,) + by_channel.shape[1:], BF16),
            pltpu.VMEM((1, chans), jnp.int32),
            pltpu.VMEM((1, chans), jnp.int32),
            pltpu.VMEM((n_tmpl, chans, width), BF16),
            pltpu.VMEM((n_sta, GROUPS, LANES), F32),
            pltpu.VMEM((n_tmpl, rows, LANES), F32),
            pltpu.VMEM((rows, depth), F32),
            pltpu.VMEM((rows // 8, 8 * STEP, depth), BF16),
            pltpu.VMEM((SPAN + 2, rows // 8, 8 * SUB, LANES), BF16),
            pltpu.VMEM((SPAN + 3, rows, LANES), BF16),
            pltpu.VMEM((SPAN, rows, LANES), F32),
            pltpu.VMEM((blocks, GROUPS, LANES), BF16),
            pltpu.VMEM((n_sta, blocks // n_sta, GROUPS, LANES), BF16),
            pltpu.VMEM((8, LANES), jnp.int32),
            pltpu.SemaphoreType.DMA((LIB_COPIES,)),
            pltpu.SemaphoreType.DMA,
            pltpu.SemaphoreType.DMA,
            pltpu.SemaphoreType.DMA,
            pltpu.SemaphoreType.DMA((n_tmpl,)),
            pltpu.SemaphoreType.DMA((n_tmpl,)),
            pltpu.SemaphoreType.DMA((n_sta,)),
            pltpu.SemaphoreType.DMA((n_sta,)),
            pltpu.SemaphoreType.DMA((n_sta,)),
            pltpu.SemaphoreType.DMA((n_sta,)),
        ],
        compiler_params=pltpu.CompilerParams(
            collective_id=0, has_side_effects=True, vmem_limit_bytes=56 * 1024 * 1024
        ),
    )(window, by_channel, library_index, moveout, group_of.reshape(1, -1))


def solution(mesh):
    in_specs = (P("sta", "tmpl"), P(None, "sta", None), P("tmpl"), P("tmpl", "sta"), P("sta"))
    body = functools.partial(on_device, mesh.shape["tmpl"], mesh.shape["sta"])
    return jax.shard_map(
        body, mesh=mesh, in_specs=in_specs, out_specs=P("tmpl", None, "sta"), check_vma=False
    )
```
